32 devices in a mesh: leaf: 4 (over z), row: 2 (over core), col: 4 (over y, x).
Axes of the slice: x: 2, y: 2, z: 4, core: 2. Of those that a mesh axis runs over, the one named last changes fastest.
Arguments:
- leaf_rhs: float32 [4, 2048, 256], P('leaf'), may hold values from -6 to 6
- root_rhs: float32 [8, 128, 256], P(None, None, ('row', 'col')), may hold values from -6 to 6
- leaf_inverse: float32 [4, 2048, 2048], P('leaf', ('row', 'col')), as said below
- coupling: float32 [4, 8, 128, 2048], P('leaf', None, None, ('row', 'col')), may hold values from -0.0625 to 0.0625
- coupled: int32 [4, 8], P('leaf'), may hold values 0 or 1
- root_inverse: float32 [8, 128, 128], replicated
- root_lower: float32 [8, 8, 128, 128], replicated, may hold values from -0.09375 to 0.09375
Outputs:
- leaf_solution: float32 [4, 2048, 256], P('leaf', ('row', 'col'))
- root_solution: float32 [8, 128, 256], P(None, None, ('row', 'col'))
The draws below stay inside these ranges and needn't reach their ends.
Inputs may be any that keep to these rules, and one draw needn't show every extreme that they name: leaf_inverse[i] and root_inverse[k] are lower triangular with positive diagonals.
All inputs are finite; a program needn't handle non-finite values. No bound on the sum of `coupled` on one device may be relied on, other than what follows from the above.
Results may differ from the reference program's by a relative error of at most 0.0001.
Values sent between devices are 32-bit elements; how exact they have to be, the bound alone decides.
A program may use at most 64 MiB of HBM per device.

```python
import jax
import jax.numpy as jnp
from jax import lax

NRHS = 256
W = 128
SEPS = 8
NL = 2048
LEAVES = 4


def assemble(offdiag, key, order):
    rows = lax.broadcasted_iota(jnp.int32, (order, order), 0)
    cols = lax.broadcasted_iota(jnp.int32, (order, order), 1)
    diagonal = jnp.exp(jax.random.uniform(key, offdiag.shape[:-1], jnp.float32, -0.7, 0.7))
    scaled = offdiag / jnp.sqrt(jnp.float32(order))
    lower = jnp.where(rows > cols, scaled, 0.0)
    return lower + jnp.where(rows == cols, diagonal[..., :, None], 0.0)


def draw_leaf_inverse(key, part):
    key = jax.random.fold_in(key, 11)
    first, second = jax.random.split(key)
    offdiag = jax.random.normal(first, (LEAVES, NL, NL), jnp.float32) * 0.7
    return assemble(offdiag, second, NL)


def draw_root_inverse(key, part):
    key = jax.random.fold_in(key, 23)
    first, second = jax.random.split(key)
    offdiag = jax.random.normal(first, (SEPS, W, W), jnp.float32) * 0.7
    return assemble(offdiag, second, W)


def plant(entries, own_key, smallest, top_value):
    place = [jax.random.randint(jax.random.fold_in(own_key, axis), (), 0, length) for axis, length in enumerate(entries.shape)]
    longest = entries.shape.index(max(entries.shape))
    neighbour = place[:longest] + [(place[longest] + 1) % entries.shape[longest]] + place[longest + 1:]
    return entries.at[tuple(place)].set(smallest).at[tuple(neighbour)].set(top_value)


def block_scale(rng, shape, pieces, low, largest):
    loudness = 1.0
    for dim, parts in pieces:
        steps = jax.random.uniform(jax.random.fold_in(jax.random.fold_in(rng, 6), dim), (parts,), jnp.float32, low / len(pieces), largest / len(pieces))
        loudness = loudness * jnp.repeat(jnp.exp(steps), shape[dim] // parts).reshape((-1,) + (1,) * (len(shape) - 1 - dim))
    return loudness


def scatter_about(stream_key, shape, width, bound, pieces=(), kind=jnp.bfloat16):
    gain = block_scale(stream_key, shape, pieces, -0.22, 0.18) if pieces else 1.0
    drawn = jax.random.normal(stream_key, shape, jnp.float32) * width * gain
    return jnp.minimum(jnp.maximum(drawn, -bound), bound).astype(kind)


def setup_inputs(seed: int = 0) -> dict:
    streams_of = jax.random.split(jax.random.key(seed), 8)
    leaf_rhs = scatter_about(streams_of[0], (LEAVES, NL, NRHS), 1.0, 6.0, ((0, 4),), jnp.float32)
    root_rhs = scatter_about(streams_of[1], (SEPS, W, NRHS), 1.0, 6.0, ((2, 8),), jnp.float32)
    leaf_inverse = draw_leaf_inverse(jax.random.fold_in(streams_of[7], 71), 0)
    coupling = scatter_about(streams_of[3], (LEAVES, SEPS, W, NL), (LEAVES * NL) ** -0.5, 0.0625, ((0, 4), (3, 8)), jnp.float32)
    coupled = plant((jax.random.randint(streams_of[4], (LEAVES, SEPS), 0, 2) < 1).astype(jnp.int32), jax.random.fold_in(streams_of[4], 1), 0, 1)
    root_inverse = draw_root_inverse(jax.random.fold_in(streams_of[7], 71), 0)
    root_lower = scatter_about(streams_of[6], (SEPS, SEPS, W, W), (4 * W * SEPS) ** -0.5, 0.09375, (), jnp.float32)
    return dict(leaf_rhs=leaf_rhs, root_rhs=root_rhs, leaf_inverse=leaf_inverse, coupling=coupling, coupled=coupled, root_inverse=root_inverse, root_lower=root_lower)


def reference(leaf_rhs, root_rhs, leaf_inverse, coupling, coupled, root_inverse, root_lower):
    high = lax.Precision.HIGHEST
    pattern = coupled.astype(jnp.float32)
    leaf_forward = jnp.einsum('inm,imq->inq', leaf_inverse, leaf_rhs, precision=high)

    def add_leaf(total, index):
        blocks = coupling[index]
        term = jnp.einsum('kwn,nq->kwq', blocks, leaf_forward[index], precision=high)
        return total + pattern[index][:, None, None] * term, None

    start = jnp.zeros((SEPS, W, NRHS), jnp.float32)
    gathered_update, _ = lax.scan(add_leaf, start, jnp.arange(LEAVES, dtype=jnp.int32))

    def forward(step, solved):
        others = jnp.einsum('jwv,jvq->wq', root_lower[step], solved, precision=high)
        segment = jnp.dot(root_inverse[step], root_rhs[step] - gathered_update[step] - others, precision=high)
        return solved.at[step].set(segment)

    root_forward = lax.fori_loop(0, SEPS, forward, jnp.zeros((SEPS, W, NRHS), jnp.float32))

    def backward(count, solved):
        step = SEPS - 1 - count
        column = root_lower[:, step]
        others = jnp.einsum('jvw,jvq->wq', column, solved, precision=high)
        segment = jnp.dot(root_inverse[step].T, root_forward[step] - others, precision=high)
        return solved.at[step].set(segment)

    root_solution = lax.fori_loop(0, SEPS, backward, jnp.zeros((SEPS, W, NRHS), jnp.float32))

    def leaf_back(index):
        weighted = root_solution * pattern[index][:, None, None]
        update = jnp.einsum('kwn,kwq->nq', coupling[index], weighted, precision=high)
        residual = leaf_forward[index] - update
        return jnp.dot(leaf_inverse[index].T, residual, precision=high)

    leaf_solution = lax.map(leaf_back, jnp.arange(LEAVES, dtype=jnp.int32))
    return leaf_solution, root_solution
```

```python
import functools

import jax
import jax.numpy as jnp
from jax import lax
from jax.experimental import pallas as pl
from jax.experimental.pallas import tpu as pltpu
from jax.sharding import PartitionSpec as P

F32 = jnp.float32
BF16 = jnp.bfloat16
MESH = pl.DeviceIdType.MESH
NN = (((1,), (0,)), ((), ()))
NT = (((1,), (1,)), ((), ()))


def split(value):
    high = value.astype(BF16)
    return high, (value - high.astype(F32)).astype(BF16)


def mul(a, b, dims=NN):
    dot = functools.partial(lax.dot_general, dimension_numbers=dims, preferred_element_type=F32)
    return dot(a[0], b[0]) + (dot(a[0], b[1]) + dot(a[1], b[0]))


def kernel(
    sizes,
    rhs_hbm, root_rhs_hbm, inverse_hbm, coupling_hbm, coupled_ref, root_inverse_hbm, root_lower_hbm,
    leaf_out, root_out,
    rhs_v, inverse_v, coupling_v, root_rhs_v, root_inverse_v, root_lower_v,
    solved, turned, turned_hi, turned_lo, coup_hi, coup_lo, inv_hi, inv_lo,
    t_full, t_hi, t_lo,
    term, pair_in, pair_sum, cols_in, slab, slab_in, mine, gathered,
    root_all, resid_hi, resid_lo, part, part_in, part_cols,
    load_sem, rhs_sem, inv_sem,
    pair_sem, cols_sem, leaf_sem, back_sem, root_sem, root_pair_sem, fin_pair_sem, fin_sem,
):
    leaves, cols, seps, width, order, rows, nrhs = sizes
    narrow = nrhs // (2 * cols)
    groups = narrow // 8
    per = groups * seps // leaves
    step = rows
    chunks = order // step
    l = lax.axis_index("leaf")
    r = lax.axis_index("row")
    c = lax.axis_index("col")

    def turn(value, by, count):
        return lax.rem(value + by, count)

    def at_row(x):
        return {"leaf": l, "row": x, "col": c}

    def at_col(x):
        return {"leaf": l, "row": r, "col": x}

    def at_leaf(x):
        return {"leaf": x, "row": r, "col": c}

    def remote(src, dst, sem, i, where):
        return pltpu.make_async_remote_copy(
            src_ref=src, dst_ref=dst, send_sem=sem.at[0, i], recv_sem=sem.at[1, i],
            device_id=where, device_id_type=MESH,
        )

    def inv_load(m):
        return pltpu.make_async_copy(
            inverse_hbm.at[0, :, pl.ds(pl.multiple_of(m * step, 128), step)], inverse_v.at[m], inv_sem.at[m]
        )

    def rhs_load(m):
        return pltpu.make_async_copy(
            rhs_hbm.at[0, pl.ds(pl.multiple_of(m * step, 8), step), :], rhs_v.at[m], rhs_sem.at[m]
        )

    others = [
        pltpu.make_async_copy(coupling_hbm.at[0], coupling_v, load_sem.at[0]),
        pltpu.make_async_copy(root_inverse_hbm, root_inverse_v, load_sem.at[1]),
        pltpu.make_async_copy(root_rhs_hbm, root_rhs_v, load_sem.at[2]),
        pltpu.make_async_copy(root_lower_hbm, root_lower_v, load_sem.at[3]),
    ]
    for m in range(chunks):
        inv_load(m).start()
        rhs_load(m).start()
    for copy in others:
        copy.start()

    barrier = pltpu.get_barrier_semaphore()
    pl.semaphore_signal(barrier, inc=1, device_id=at_row(1 - r), device_id_type=MESH)
    for o in range(1, cols):
        pl.semaphore_signal(barrier, inc=1, device_id=at_col(turn(c, o, cols)), device_id_type=MESH)

    @pl.loop(1, leaves)
    def _(o):
        pl.semaphore_signal(barrier, inc=1, device_id=at_leaf(turn(l, o, leaves)), device_id_type=MESH)

    solved[...] = jnp.zeros_like(solved)

    @pl.loop(0, chunks)
    def _(m):
        inv_load(m).wait()
        rhs_load(m).wait()
        solved[...] += mul(split(inverse_v[m]), split(rhs_v[m]))

    turned[...] = solved[...].T
    hi, lo = split(turned[...])
    turned_hi[...] = hi
    turned_lo[...] = lo
    others[0].wait()
    for k in range(seps):
        hi, lo = split(coupling_v[k] * coupled_ref[0, k].astype(F32))
        coup_hi[k] = hi
        coup_lo[k] = lo

    def make_term(half):
        at = pl.ds(pl.multiple_of(half * (nrhs // 2), 128), nrhs // 2)
        left = (turned_hi[at, :], turned_lo[at, :])

        @pl.loop(0, seps)
        def _(k):
            value = mul(left, (coup_hi[k], coup_lo[k]), NT)
            term[half, :, :, k] = value.reshape(cols, groups, 8, width)

    make_term(1 - r)
    pl.semaphore_wait(barrier, cols + leaves - 1)
    pair_copy = remote(term.at[1 - r], pair_in, pair_sem, 0, at_row(1 - r))
    pair_copy.start()
    make_term(r)
    pair_copy.wait()

    cols_copies = []
    for o in range(1, cols):
        to = turn(c, o, cols)
        pair_sum[to] = term[r, to] + pair_in[to]
        copy = remote(pair_sum.at[to], cols_in.at[o - 1], cols_sem, o - 1, at_col(to))
        copy.start()
        cols_copies.append(copy)
    pair_sum[c] = term[r, c] + pair_in[c]

    others[1].wait()
    others[3].wait()
    for k in range(seps):
        at = pl.ds(k * width, width)
        inv_k = root_inverse_v[k]
        if k:
            low = jnp.concatenate([root_lower_v[k, j] for j in range(k)], axis=1)
            known = (t_hi[0:k * width, 0:k * width], t_lo[0:k * width, 0:k * width])
            row = -mul(split(inv_k), split(mul(split(low), known)))
            hi, lo = split(row)
            t_hi[at, 0:k * width] = hi
            t_lo[at, 0:k * width] = lo
        hi, lo = split(inv_k)
        t_hi[at, at] = hi
        t_lo[at, at] = lo
        if k + 1 < seps:
            rest = pl.ds((k + 1) * width, (seps - 1 - k) * width)
            t_hi[at, rest] = jnp.zeros((width, (seps - 1 - k) * width), BF16)
            t_lo[at, rest] = jnp.zeros((width, (seps - 1 - k) * width), BF16)

    total = pair_sum[c]
    for o in range(1, cols):
        cols_copies[o - 1].wait()
        total = total + cols_in[o - 1]
    slab[...] = total.reshape(groups * seps, 8, width)

    def piece(x):
        return pl.ds(x * per, per)

    def leaf_copy(o):
        to = turn(l, o, leaves)
        return remote(slab.at[piece(to)], slab_in.at[o - 1], leaf_sem, o - 1, at_leaf(to))

    def back_copy(o):
        to = turn(l, o, leaves)
        return remote(mine, gathered.at[piece(l)], back_sem, o - 1, at_leaf(to))

    @pl.loop(1, leaves)
    def _(o):
        leaf_copy(o).start()

    mine[...] = slab[piece(l)]

    @pl.loop(0, chunks)
    def _(m):
        hi, lo = split(inverse_v[m].T)
        inv_hi[m] = hi
        inv_lo[m] = lo

    @pl.loop(1, leaves)
    def _(o):
        leaf_copy(o).wait()
        mine[...] += slab_in[o - 1]

    @pl.loop(1, leaves)
    def _(o):
        back_copy(o).start()

    gathered[piece(l)] = mine[...]
    others[2].wait()
    base = jnp.concatenate([root_rhs_v[k].T for k in range(seps)], axis=1)

    @pl.loop(1, leaves)
    def _(o):
        back_copy(o).wait()

    update = jnp.concatenate(
        [gathered[...].reshape(groups, seps, 8, width)[:, k].reshape(narrow, width) for k in range(seps)], axis=1
    )
    pending = base - update
    block = 2 * width
    blocks = seps // 2
    hi, lo = split(pending)
    forward = []
    for b in range(blocks):
        at = pl.ds(b * block, block)
        upto = (b + 1) * block
        forward.append(
            mul((hi[:, :upto], lo[:, :upto]), (t_hi[at, 0:upto], t_lo[at, 0:upto]), NT)
        )
    hi, lo = split(jnp.concatenate(forward, axis=1))
    solution_parts = []
    for b in range(blocks):
        at = pl.ds(b * block, block)
        rest = pl.ds(b * block, (blocks - b) * block)
        solution_parts.append(
            mul((hi[:, b * block:], lo[:, b * block:]), (t_hi[rest, at], t_lo[rest, at]), NN)
        )
    for k in range(seps):
        part_k = solution_parts[k // 2][:, (k % 2) * width:(k % 2 + 1) * width]
        root_all[r, c, :, k] = part_k.reshape(groups, 8, width)

    root_copies = []
    for o in range(1, cols):
        to = turn(c, o, cols)
        copy = remote(root_all.at[r, c], root_all.at[r, c], root_sem, o - 1, at_col(to))
        copy.start()
        root_copies.append(copy)

    def root_pair(i, which):
        return remote(root_all.at[r, which], root_all.at[r, which], root_pair_sem, i, at_row(1 - r))

    pair_copies = [root_pair(0, c)]
    pair_copies[0].start()
    for k in range(seps):
        part_k = solution_parts[k // 2][:, (k % 2) * width:(k % 2 + 1) * width]
        root_out[k] = part_k.T
    for o in range(1, cols):
        root_copies[o - 1].wait()
        copy = root_pair(o, turn(c, cols - o, cols))
        copy.start()
        pair_copies.append(copy)

    def make_resid(half):
        at = pl.ds(pl.multiple_of(half * (nrhs // 2), 128), nrhs // 2)
        value = root_all[half]
        left = split(jnp.concatenate([value[:, :, k].reshape(nrhs // 2, width) for k in range(seps)], axis=1))
        right = (coup_hi[...].reshape(seps * width, rows), coup_lo[...].reshape(seps * width, rows))
        return turned[at, :] - mul(left, right)

    turned[pl.ds(pl.multiple_of(r * (nrhs // 2), 128), nrhs // 2), :] = make_resid(r)
    for copy in pair_copies:
        copy.wait()
    other = 1 - r
    turned[pl.ds(pl.multiple_of(other * (nrhs // 2), 128), nrhs // 2), :] = make_resid(other)
    hi, lo = split(turned[...].T)
    resid_hi[...] = hi
    resid_lo[...] = lo

    def make_part(b):
        part[b] = mul((inv_hi[b], inv_lo[b]), (resid_hi[...], resid_lo[...]))

    def fin_pair(o):
        to = turn(c, o, cols)
        return remote(part.at[to], part_in.at[to], fin_pair_sem, o, at_row(0))

    def fin(o):
        to = turn(c, o, cols)
        return remote(part.at[r * cols + to], part_cols.at[o - 1], fin_sem, o - 1, at_col(to))

    @pl.when(r == 1)
    def _():
        for i in range(cols):
            o = (i + 1) % cols
            make_part(turn(c, o, cols))
            fin_pair(o).start()
        for i in range(cols):
            o = (i + 1) % cols
            to = turn(c, o, cols)

            @pl.when(to <= c)
            def _():
                make_part(cols + to)
                if o:
                    fin(o).start()
        for o in range(cols):
            fin_pair(o).wait_send()
        for o in range(1, cols):
            to = turn(c, o, cols)

            @pl.when(to < c)
            def _():
                fin(o).wait_send()

        leaf_out[0] = part[cols + c]
        for o in range(1, cols):
            source = turn(c, cols - o, cols)

            @pl.when(source > c)
            def _():
                fin(o).wait_recv()
                leaf_out[0] += part_cols[o - 1]

    @pl.when(r == 0)
    def _():
        for b in range(cols):
            make_part(b)
        for i in range(cols):
            o = (i + 1) % cols
            to = turn(c, o, cols)
            fin_pair_in = pltpu.make_async_remote_copy(
                src_ref=part.at[to], dst_ref=part_in.at[to],
                send_sem=fin_pair_sem.at[0, o], recv_sem=fin_pair_sem.at[1, o],
                device_id=at_row(1), device_id_type=MESH,
            )
            fin_pair_in.wait_recv()
            part[to] += part_in[to]
            if o:
                fin(o).start()
        leaf_out[0] = part[c]
        for o in range(1, cols):
            fin(o).wait_send()
            fin(o).wait_recv()
            leaf_out[0] += part_cols[o - 1]


def per_device(sizes, leaf_rhs, root_rhs, leaf_inverse, coupling, coupled, root_inverse, root_lower):
    leaves, cols, seps, width, order, rows, nrhs = sizes
    narrow = nrhs // (2 * cols)
    groups = narrow // 8
    per = groups * seps // leaves
    chunks = order // rows
    slab_shape = (groups, seps, 8, width)
    any_space = pl.BlockSpec(memory_space=pl.ANY)
    vmem = pl.BlockSpec(memory_space=pltpu.VMEM)
    smem = pl.BlockSpec(memory_space=pltpu.SMEM)
    total = seps * width
    V = pltpu.VMEM
    sem = lambda *shape: pltpu.SemaphoreType.DMA(shape)
    scratch = [
        V((chunks, rows, nrhs), F32), V((chunks, rows, rows), F32), V((seps, width, rows), F32),
        V((seps, width, narrow), F32), V((seps, width, width), F32), V((seps, seps, width, width), F32),
        V((rows, nrhs), F32), V((nrhs, rows), F32), V((nrhs, rows), BF16), V((nrhs, rows), BF16),
        V((seps, width, rows), BF16), V((seps, width, rows), BF16),
        V((chunks, rows, rows), BF16), V((chunks, rows, rows), BF16),
        V((8, width), F32), V((total, total), BF16), V((total, total), BF16),
        V((2, cols) + slab_shape, F32), V((cols,) + slab_shape, F32), V((cols,) + slab_shape, F32),
        V((cols - 1,) + slab_shape, F32), V((groups * seps, 8, width), F32),
        V((leaves - 1, per, 8, width), F32), V((per, 8, width), F32), V((groups * seps, 8, width), F32),
        V((2, cols) + slab_shape, F32), V((rows, nrhs), BF16), V((rows, nrhs), BF16),
        V((2 * cols, rows, nrhs), F32), V((cols, rows, nrhs), F32), V((cols - 1, rows, nrhs), F32),
        sem(4), sem(chunks), sem(chunks),
        sem(2, 1), sem(2, cols - 1), sem(2, leaves - 1), sem(2, leaves - 1),
        sem(2, cols - 1), sem(2, cols), sem(2, cols), sem(2, cols - 1),
    ]
    return pl.pallas_call(
        functools.partial(kernel, sizes),
        out_shape=(
            jax.ShapeDtypeStruct((1, rows, nrhs), F32),
            jax.ShapeDtypeStruct((seps, width, narrow), F32),
        ),
        in_specs=[any_space, any_space, any_space, any_space, smem, any_space, any_space],
        out_specs=(vmem, vmem),
        scratch_shapes=scratch,
        compiler_params=pltpu.CompilerParams(
            collective_id=0, has_side_effects=True, vmem_limit_bytes=56 * 1024 * 1024
        ),
    )(leaf_rhs, root_rhs, leaf_inverse, coupling, coupled, root_inverse, root_lower)


def solution(mesh):
    in_specs = (
        P("leaf", None, None),
        P(None, None, ("row", "col")),
        P("leaf", ("row", "col"), None),
        P("leaf", None, None, ("row", "col")),
        P("leaf", None),
        P(),
        P(),
    )
    out_specs = (P("leaf", ("row", "col"), None), P(None, None, ("row", "col")))
    leaves, cols = mesh.shape["leaf"], mesh.shape["col"]

    def run(leaf_rhs, root_rhs, leaf_inverse, coupling, coupled, root_inverse, root_lower):
        seps, width, nrhs = root_rhs.shape
        order = leaf_rhs.shape[1]
        sizes = (leaves, cols, seps, width, order, order // (2 * cols), nrhs)
        mapped = jax.shard_map(
            functools.partial(per_device, sizes), mesh=mesh, in_specs=in_specs, out_specs=out_specs,
            check_vma=False,
        )
        return mapped(leaf_rhs, root_rhs, leaf_inverse, coupling, coupled, root_inverse, root_lower)

    return run
```

```python
import functools

import jax
import jax.numpy as jnp
from jax import lax
from jax.experimental import pallas as pl
from jax.experimental.pallas import tpu as pltpu
from jax.sharding import PartitionSpec as P

F32 = jnp.float32
BF16 = jnp.bfloat16
MESH = pl.DeviceIdType.MESH
NN = (((1,), (0,)), ((), ()))
NT = (((1,), (1,)), ((), ()))


def split(value):
    high = value.astype(BF16)
    return high, (value - high.astype(F32)).astype(BF16)


def mul(a, b, dims=NN):
    dot = functools.partial(lax.dot_general, dimension_numbers=dims, preferred_element_type=F32)
    return dot(a[0], b[0]) + (dot(a[0], b[1]) + dot(a[1], b[0]))


def halves_of(groups, seps, leaves):
    return 2 if (groups * seps // 2) % leaves == 0 else 1


def kernel(
    sizes,
    rhs_hbm, root_rhs_hbm, inverse_hbm, coupling_hbm, coupled_ref, root_inverse_hbm, root_lower_hbm,
    leaf_out, root_out,
    rhs_v, inverse_v, coupling_v, root_rhs_v, root_inverse_v, root_lower_v,
    solved, turned, turned_hi, turned_lo, coup_hi, coup_lo, inv_hi, inv_lo,
    t_hi, t_lo,
    term, pair_in, pair_sum, cols_in, slab, slab_in, mine, gathered,
    root_all, resid_hi, resid_lo, part, part_in, part_cols,
    load_sem, rhs_sem, inv_sem,
    pair_sem, cols_sem, leaf_sem, back_sem, root_sem, root_pair_sem, fin_pair_sem, fin_sem,
):
    leaves, cols, seps, width, order, rows, nrhs = sizes
    narrow = nrhs // (2 * cols)
    groups = narrow // 8
    halves = halves_of(groups, seps, leaves)
    some = seps // halves
    per = groups * some // leaves
    step = rows
    chunks = order // step
    l = lax.axis_index("leaf")
    r = lax.axis_index("row")
    c = lax.axis_index("col")

    def turn(value, by, count):
        return lax.rem(value + by, count)

    def at_row(x):
        return {"leaf": l, "row": x, "col": c}

    def at_col(x):
        return {"leaf": l, "row": r, "col": x}

    def at_leaf(x):
        return {"leaf": x, "row": r, "col": c}

    def remote(src, dst, sem, i, where):
        return pltpu.make_async_remote_copy(
            src_ref=src, dst_ref=dst, send_sem=sem.at[0, i], recv_sem=sem.at[1, i],
            device_id=where, device_id_type=MESH,
        )

    def inv_load(m):
        return pltpu.make_async_copy(
            inverse_hbm.at[0, :, pl.ds(pl.multiple_of(m * step, 128), step)], inverse_v.at[m], inv_sem.at[m]
        )

    def rhs_load(m):
        return pltpu.make_async_copy(
            rhs_hbm.at[0, pl.ds(pl.multiple_of(m * step, 8), step), :], rhs_v.at[m], rhs_sem.at[m]
        )

    others = [
        pltpu.make_async_copy(coupling_hbm.at[0], coupling_v, load_sem.at[0]),
        pltpu.make_async_copy(root_inverse_hbm, root_inverse_v, load_sem.at[1]),
        pltpu.make_async_copy(root_rhs_hbm, root_rhs_v, load_sem.at[2]),
        pltpu.make_async_copy(root_lower_hbm, root_lower_v, load_sem.at[3]),
    ]
    for m in range(chunks):
        inv_load(m).start()
        rhs_load(m).start()
    for copy in others:
        copy.start()

    barrier = pltpu.get_barrier_semaphore()
    pl.semaphore_signal(barrier, inc=1, device_id=at_row(1 - r), device_id_type=MESH)
    for o in range(1, cols):
        pl.semaphore_signal(barrier, inc=1, device_id=at_col(turn(c, o, cols)), device_id_type=MESH)

    @pl.loop(1, leaves)
    def _(o):
        pl.semaphore_signal(barrier, inc=1, device_id=at_leaf(turn(l, o, leaves)), device_id_type=MESH)

    solved[...] = jnp.zeros_like(solved)

    @pl.loop(0, chunks)
    def _(m):
        inv_load(m).wait()
        rhs_load(m).wait()
        solved[...] += mul(split(inverse_v[m]), split(rhs_v[m]))

    turned[...] = solved[...].T
    hi, lo = split(turned[...])
    turned_hi[...] = hi
    turned_lo[...] = lo
    others[0].wait()
    for k in range(seps):
        hi, lo = split(coupling_v[k] * coupled_ref[0, k].astype(F32))
        coup_hi[k] = hi
        coup_lo[k] = lo

    def make_term(half, h):
        at = pl.ds(pl.multiple_of(half * (nrhs // 2), 128), nrhs // 2)
        left = (turned_hi[at, :], turned_lo[at, :])

        @pl.loop(0, some)
        def _(k):
            value = mul(left, (coup_hi[h * some + k], coup_lo[h * some + k]), NT)
            term[half, h, :, :, k] = value.reshape(cols, groups, 8, width)

    pair_starts = []
    for h in range(halves):
        make_term(1 - r, h)
        if h == 0:
            pl.semaphore_wait(barrier, cols + leaves - 1)
        copy = remote(term.at[1 - r, h], pair_in.at[h], pair_sem, h, at_row(1 - r))
        copy.start()
        pair_starts.append(copy)

    cols_copies = []
    for h in range(halves):
        make_term(r, h)
        pair_starts[h].wait()
        for o in range(1, cols):
            to = turn(c, o, cols)
            pair_sum[h, to] = term[r, h, to] + pair_in[h, to]
            i = h * (cols - 1) + o - 1
            copy = remote(pair_sum.at[h, to], cols_in.at[i], cols_sem, i, at_col(to))
            copy.start()
            cols_copies.append(copy)
        pair_sum[h, c] = term[r, h, c] + pair_in[h, c]

    others[1].wait()
    others[3].wait()

    def make_t(k):
        at = pl.ds(k * width, width)
        inv_k = root_inverse_v[k]
        if k:
            low = jnp.concatenate([root_lower_v[k, j] for j in range(k)], axis=1)
            known = (t_hi[0:k * width, 0:k * width], t_lo[0:k * width, 0:k * width])
            row = -mul(split(inv_k), split(mul(split(low), known)))
            hi, lo = split(row)
            t_hi[at, 0:k * width] = hi
            t_lo[at, 0:k * width] = lo
        hi, lo = split(inv_k)
        t_hi[at, at] = hi
        t_lo[at, at] = lo
        if k + 1 < seps:
            rest = pl.ds((k + 1) * width, (seps - 1 - k) * width)
            t_hi[at, rest] = jnp.zeros((width, (seps - 1 - k) * width), BF16)
            t_lo[at, rest] = jnp.zeros((width, (seps - 1 - k) * width), BF16)

    def piece(x):
        return pl.ds(x * per, per)

    def leaf_copy(h, o):
        to = turn(l, o, leaves)
        i = h * (leaves - 1) + o - 1
        return remote(slab.at[h, piece(to)], slab_in.at[i], leaf_sem, i, at_leaf(to))

    def back_copy(h, o):
        to = turn(l, o, leaves)
        i = h * (leaves - 1) + o - 1
        return remote(mine.at[h], gathered.at[h, piece(l)], back_sem, i, at_leaf(to))

    done = 0
    for h in range(halves):
        upto = seps if h == halves - 1 else min(5, seps)
        if h == halves - 1 and halves > 1:
            upto = seps - 1
        for k in range(done, upto):
            make_t(k)
        done = upto
        total = pair_sum[h, c]
        for o in range(1, cols):
            cols_copies[h * (cols - 1) + o - 1].wait()
            total = total + cols_in[h * (cols - 1) + o - 1]
        slab[h] = total.reshape(groups * some, 8, width)

        @pl.loop(1, leaves)
        def _(o):
            leaf_copy(h, o).start()

        mine[h] = slab[h, piece(l)]

    for k in range(done, seps):
        make_t(k)

    for h in range(halves):
        @pl.loop(1, leaves)
        def _(o):
            leaf_copy(h, o).wait()
            mine[h] += slab_in[h * (leaves - 1) + o - 1]

        @pl.loop(1, leaves)
        def _(o):
            back_copy(h, o).start()

        gathered[h, piece(l)] = mine[h]
        if h == 0:
            @pl.loop(0, chunks)
            def _(m):
                hi, lo = split(inverse_v[m].T)
                inv_hi[m] = hi
                inv_lo[m] = lo

    others[2].wait()
    base = jnp.concatenate([root_rhs_v[k] for k in range(seps)], axis=1)
    updates = []
    for h in range(halves):
        @pl.loop(1, leaves)
        def _(o):
            back_copy(h, o).wait()

        value = gathered[h].reshape(groups, some, 8, width)
        updates += [value[:, k].reshape(narrow, width) for k in range(some)]
    update = jnp.concatenate(updates, axis=1)
    pending = base - update
    block = 2 * width
    blocks = seps // 2
    hi, lo = split(pending)
    forward = []
    for b in range(blocks):
        at = pl.ds(b * block, block)
        upto = (b + 1) * block
        forward.append(
            mul((hi[:, :upto], lo[:, :upto]), (t_hi[at, 0:upto], t_lo[at, 0:upto]), NT)
        )
    hi, lo = split(jnp.concatenate(forward, axis=1))
    solution_parts = []
    for b in range(blocks):
        at = pl.ds(b * block, block)
        rest = pl.ds(b * block, (blocks - b) * block)
        solution_parts.append(
            mul((hi[:, b * block:], lo[:, b * block:]), (t_hi[rest, at], t_lo[rest, at]), NN)
        )
    for k in range(seps):
        part_k = solution_parts[k // 2][:, (k % 2) * width:(k % 2 + 1) * width]
        root_all[r, c, :, k] = part_k.reshape(groups, 8, width)

    root_copies = []
    for o in range(1, cols):
        to = turn(c, o, cols)
        copy = remote(root_all.at[r, c], root_all.at[r, c], root_sem, o - 1, at_col(to))
        copy.start()
        root_copies.append(copy)

    def root_pair(i, which):
        return remote(root_all.at[r, which], root_all.at[r, which], root_pair_sem, i, at_row(1 - r))

    pair_copies = [root_pair(0, c)]
    pair_copies[0].start()
    for k in range(seps):
        part_k = solution_parts[k // 2][:, (k % 2) * width:(k % 2 + 1) * width]
        root_out[k] = part_k
    for o in range(1, cols):
        root_copies[o - 1].wait()
        copy = root_pair(o, turn(c, cols - o, cols))
        copy.start()
        pair_copies.append(copy)

    def make_resid(half):
        at = pl.ds(pl.multiple_of(half * (nrhs // 2), 128), nrhs // 2)
        value = root_all[half]
        left = split(jnp.concatenate([value[:, :, k].reshape(nrhs // 2, width) for k in range(seps)], axis=1))
        right = (coup_hi[...].reshape(seps * width, rows), coup_lo[...].reshape(seps * width, rows))
        return turned[at, :] - mul(left, right)

    turned[pl.ds(pl.multiple_of(r * (nrhs // 2), 128), nrhs // 2), :] = make_resid(r)
    for copy in pair_copies:
        copy.wait()
    other = 1 - r
    turned[pl.ds(pl.multiple_of(other * (nrhs // 2), 128), nrhs // 2), :] = make_resid(other)
    hi, lo = split(turned[...].T)
    resid_hi[...] = hi
    resid_lo[...] = lo

    def make_part(b):
        part[b] = mul((inv_hi[b], inv_lo[b]), (resid_hi[...], resid_lo[...]))

    def fin_pair(o):
        to = turn(c, o, cols)
        return remote(part.at[to], part_in.at[to], fin_pair_sem, o, at_row(0))

    def fin(o):
        to = turn(c, o, cols)
        return remote(part.at[r * cols + to], part_cols.at[o - 1], fin_sem, o - 1, at_col(to))

    @pl.when(r == 1)
    def _():
        for i in range(cols):
            o = (i + 1) % cols
            make_part(turn(c, o, cols))
            fin_pair(o).start()
        for i in range(cols):
            o = (i + 1) % cols
            to = turn(c, o, cols)

            @pl.when(to <= c)
            def _():
                make_part(cols + to)
                if o:
                    fin(o).start()
        for o in range(cols):
            fin_pair(o).wait_send()
        for o in range(1, cols):
            to = turn(c, o, cols)

            @pl.when(to < c)
            def _():
                fin(o).wait_send()

        leaf_out[0] = part[cols + c]
        for o in range(1, cols):
            source = turn(c, cols - o, cols)

            @pl.when(source > c)
            def _():
                fin(o).wait_recv()
                leaf_out[0] += part_cols[o - 1]

    @pl.when(r == 0)
    def _():
        for b in range(cols):
            make_part(b)
        for i in range(cols):
            o = (i + 1) % cols
            to = turn(c, o, cols)
            fin_pair_in = pltpu.make_async_remote_copy(
                src_ref=part.at[to], dst_ref=part_in.at[to],
                send_sem=fin_pair_sem.at[0, o], recv_sem=fin_pair_sem.at[1, o],
                device_id=at_row(1), device_id_type=MESH,
            )
            fin_pair_in.wait_recv()
            part[to] += part_in[to]
            if o:
                fin(o).start()
        leaf_out[0] = part[c]
        for o in range(1, cols):
            fin(o).wait_send()
            fin(o).wait_recv()
            leaf_out[0] += part_cols[o - 1]


def per_device(sizes, leaf_rhs, root_rhs, leaf_inverse, coupling, coupled, root_inverse, root_lower):
    leaves, cols, seps, width, order, rows, nrhs = sizes
    narrow = nrhs // (2 * cols)
    groups = narrow // 8
    halves = halves_of(groups, seps, leaves)
    some = seps // halves
    per = groups * some // leaves
    chunks = order // rows
    slab_shape = (groups, seps, 8, width)
    half_shape = (groups, some, 8, width)
    any_space = pl.BlockSpec(memory_space=pl.ANY)
    vmem = pl.BlockSpec(memory_space=pltpu.VMEM)
    smem = pl.BlockSpec(memory_space=pltpu.SMEM)
    total = seps * width
    V = pltpu.VMEM
    sem = lambda *shape: pltpu.SemaphoreType.DMA(shape)
    scratch = [
        V((chunks, rows, nrhs), F32), V((chunks, rows, rows), F32), V((seps, width, rows), F32),
        V((seps, narrow, width), F32), V((seps, width, width), F32), V((seps, seps, width, width), F32),
        V((rows, nrhs), F32), V((nrhs, rows), F32), V((nrhs, rows), BF16), V((nrhs, rows), BF16),
        V((seps, width, rows), BF16), V((seps, width, rows), BF16),
        V((chunks, rows, rows), BF16), V((chunks, rows, rows), BF16),
        V((total, total), BF16), V((total, total), BF16),
        V((2, halves, cols) + half_shape, F32), V((halves, cols) + half_shape, F32),
        V((halves, cols) + half_shape, F32), V((halves * (cols - 1),) + half_shape, F32),
        V((halves, groups * some, 8, width), F32), V((halves * (leaves - 1), per, 8, width), F32),
        V((halves, per, 8, width), F32), V((halves, groups * some, 8, width), F32),
        V((2, cols) + slab_shape, F32), V((rows, nrhs), BF16), V((rows, nrhs), BF16),
        V((2 * cols, rows, nrhs), F32), V((cols, rows, nrhs), F32), V((cols - 1, rows, nrhs), F32),
        sem(4), sem(chunks), sem(chunks),
        sem(2, halves), sem(2, halves * (cols - 1)), sem(2, halves * (leaves - 1)), sem(2, halves * (leaves - 1)),
        sem(2, cols - 1), sem(2, cols), sem(2, cols), sem(2, cols - 1),
    ]
    leaf_result, root_result = pl.pallas_call(
        functools.partial(kernel, sizes),
        out_shape=(
            jax.ShapeDtypeStruct((1, rows, nrhs), F32),
            jax.ShapeDtypeStruct((seps, narrow, width), F32),
        ),
        in_specs=[any_space, any_space, any_space, any_space, smem, any_space, any_space],
        out_specs=(vmem, vmem),
        scratch_shapes=scratch,
        compiler_params=pltpu.CompilerParams(
            collective_id=0, has_side_effects=True, vmem_limit_bytes=56 * 1024 * 1024
        ),
    )(leaf_rhs, root_rhs.transpose(0, 2, 1), leaf_inverse, coupling, coupled, root_inverse, root_lower)
    return leaf_result, root_result.transpose(0, 2, 1)


def solution(mesh):
    in_specs = (
        P("leaf", None, None),
        P(None, None, ("row", "col")),
        P("leaf", ("row", "col"), None),
        P("leaf", None, None, ("row", "col")),
        P("leaf", None),
        P(),
        P(),
    )
    out_specs = (P("leaf", ("row", "col"), None), P(None, None, ("row", "col")))
    leaves, cols = mesh.shape["leaf"], mesh.shape["col"]

    def run(leaf_rhs, root_rhs, leaf_inverse, coupling, coupled, root_inverse, root_lower):
        seps, width, nrhs = root_rhs.shape
        order = leaf_rhs.shape[1]
        sizes = (leaves, cols, seps, width, order, order // (2 * cols), nrhs)
        mapped = jax.shard_map(
            functools.partial(per_device, sizes), mesh=mesh, in_specs=in_specs, out_specs=out_specs,
            check_vma=False,
        )
        return mapped(leaf_rhs, root_rhs, leaf_inverse, coupling, coupled, root_inverse, root_lower)

    return run
```

```python
import functools

import jax
import jax.numpy as jnp
from jax import lax
from jax.experimental import pallas as pl
from jax.experimental.pallas import tpu as pltpu
from jax.sharding import PartitionSpec as P

F32 = jnp.float32
BF16 = jnp.bfloat16
MESH = pl.DeviceIdType.MESH
NN = (((1,), (0,)), ((), ()))
NT = (((1,), (1,)), ((), ()))


def split(value):
    high = value.astype(BF16)
    return high, (value - high.astype(F32)).astype(BF16)


def mul(a, b, dims=NN):
    dot = functools.partial(lax.dot_general, dimension_numbers=dims, preferred_element_type=F32)
    return dot(a[0], b[0]) + (dot(a[0], b[1]) + dot(a[1], b[0]))


def halves_of(groups, seps, leaves):
    return 2 if (groups * seps // 2) % leaves == 0 else 1


def kernel(
    sizes,
    rhs_hbm, root_rhs_hbm, inverse_hbm, coupling_hbm, coupled_ref, root_inverse_hbm, root_lower_hbm,
    leaf_out, root_out,
    rhs_v, inverse_v, coupling_v, root_rhs_v, root_inverse_v, root_lower_v,
    solved, turned, turned_hi, turned_lo, coup_hi, coup_lo, inv_hi, inv_lo,
    t_hi, t_lo,
    term, pair_in, pair_sum, cols_in, slab, slab_in, mine, gathered,
    root_all, resid_hi, resid_lo, part, part_in, relay_in, part_cols,
    load_sem, rhs_sem, inv_sem,
    pair_sem, cols_sem, leaf_sem, back_sem, root_sem, root_pair_sem, fin_pair_sem, fin_sem,
):
    leaves, cols, seps, width, order, rows, nrhs = sizes
    narrow = nrhs // (2 * cols)
    groups = narrow // 8
    halves = halves_of(groups, seps, leaves)
    some = seps // halves
    per = groups * some // leaves
    step = rows
    chunks = order // step
    l = lax.axis_index("leaf")
    r = lax.axis_index("row")
    c = lax.axis_index("col")

    def turn(value, by, count):
        return lax.rem(value + by, count)

    def at_row(x):
        return {"leaf": l, "row": x, "col": c}

    def at_col(x):
        return {"leaf": l, "row": r, "col": x}

    def at_leaf(x):
        return {"leaf": x, "row": r, "col": c}

    def remote(src, dst, sem, i, where):
        return pltpu.make_async_remote_copy(
            src_ref=src, dst_ref=dst, send_sem=sem.at[0, i], recv_sem=sem.at[1, i],
            device_id=where, device_id_type=MESH,
        )

    def inv_load(m):
        return pltpu.make_async_copy(
            inverse_hbm.at[0, :, pl.ds(pl.multiple_of(m * step, 128), step)], inverse_v.at[m], inv_sem.at[m]
        )

    def rhs_load(m):
        return pltpu.make_async_copy(
            rhs_hbm.at[0, pl.ds(pl.multiple_of(m * step, 8), step), :], rhs_v.at[m], rhs_sem.at[m]
        )

    others = [
        pltpu.make_async_copy(coupling_hbm.at[0], coupling_v, load_sem.at[0]),
        pltpu.make_async_copy(root_inverse_hbm, root_inverse_v, load_sem.at[1]),
        pltpu.make_async_copy(root_rhs_hbm, root_rhs_v, load_sem.at[2]),
        pltpu.make_async_copy(root_lower_hbm, root_lower_v, load_sem.at[3]),
    ]
    for m in range(chunks):
        inv_load(m).start()
        rhs_load(m).start()
    for copy in others:
        copy.start()

    barrier = pltpu.get_barrier_semaphore()
    pl.semaphore_signal(barrier, inc=1, device_id=at_row(1 - r), device_id_type=MESH)
    for o in range(1, cols):
        pl.semaphore_signal(barrier, inc=1, device_id=at_col(turn(c, o, cols)), device_id_type=MESH)

    @pl.loop(1, leaves)
    def _(o):
        pl.semaphore_signal(barrier, inc=1, device_id=at_leaf(turn(l, o, leaves)), device_id_type=MESH)

    solved[...] = jnp.zeros_like(solved)

    @pl.loop(0, chunks)
    def _(m):
        inv_load(m).wait()
        rhs_load(m).wait()
        solved[...] += mul(split(inverse_v[m]), split(rhs_v[m]))

    turned[...] = solved[...].T
    hi, lo = split(turned[...])
    turned_hi[...] = hi
    turned_lo[...] = lo
    others[0].wait()
    for k in range(seps):
        hi, lo = split(coupling_v[k] * coupled_ref[0, k].astype(F32))
        coup_hi[k] = hi
        coup_lo[k] = lo

    def make_term(half, h):
        at = pl.ds(pl.multiple_of(half * (nrhs // 2), 128), nrhs // 2)
        left = (turned_hi[at, :], turned_lo[at, :])

        @pl.loop(0, some)
        def _(k):
            value = mul(left, (coup_hi[h * some + k], coup_lo[h * some + k]), NT)
            term[half, h, :, :, k] = value.reshape(cols, groups, 8, width)

    pair_starts = []
    for h in range(halves):
        make_term(1 - r, h)
        if h == 0:
            pl.semaphore_wait(barrier, cols + leaves - 1)
        copy = remote(term.at[1 - r, h], pair_in.at[h], pair_sem, h, at_row(1 - r))
        copy.start()
        pair_starts.append(copy)

    cols_copies = []
    for h in range(halves):
        make_term(r, h)
        pair_starts[h].wait()
        for o in range(1, cols):
            to = turn(c, o, cols)
            pair_sum[h, to] = term[r, h, to] + pair_in[h, to]
            i = h * (cols - 1) + o - 1
            copy = remote(pair_sum.at[h, to], cols_in.at[i], cols_sem, i, at_col(to))
            copy.start()
            cols_copies.append(copy)
        pair_sum[h, c] = term[r, h, c] + pair_in[h, c]

    others[1].wait()
    others[3].wait()

    def make_t(k):
        at = pl.ds(k * width, width)
        inv_k = root_inverse_v[k]
        if k:
            low = jnp.concatenate([root_lower_v[k, j] for j in range(k)], axis=1)
            known = (t_hi[0:k * width, 0:k * width], t_lo[0:k * width, 0:k * width])
            row = -mul(split(inv_k), split(mul(split(low), known)))
            hi, lo = split(row)
            t_hi[at, 0:k * width] = hi
            t_lo[at, 0:k * width] = lo
        hi, lo = split(inv_k)
        t_hi[at, at] = hi
        t_lo[at, at] = lo
        if k + 1 < seps:
            rest = pl.ds((k + 1) * width, (seps - 1 - k) * width)
            t_hi[at, rest] = jnp.zeros((width, (seps - 1 - k) * width), BF16)
            t_lo[at, rest] = jnp.zeros((width, (seps - 1 - k) * width), BF16)

    def piece(x):
        return pl.ds(x * per, per)

    def leaf_copy(h, o):
        to = turn(l, o, leaves)
        i = h * (leaves - 1) + o - 1
        return remote(slab.at[h, piece(to)], slab_in.at[i], leaf_sem, i, at_leaf(to))

    def back_copy(h, o):
        to = turn(l, o, leaves)
        i = h * (leaves - 1) + o - 1
        return remote(mine.at[h], gathered.at[h, piece(l)], back_sem, i, at_leaf(to))

    done = 0
    for h in range(halves):
        upto = seps if h == halves - 1 else min(5, seps)
        if h == halves - 1 and halves > 1:
            upto = seps - 1
        for k in range(done, upto):
            make_t(k)
        done = upto
        total = pair_sum[h, c]
        for o in range(1, cols):
            cols_copies[h * (cols - 1) + o - 1].wait()
            total = total + cols_in[h * (cols - 1) + o - 1]
        slab[h] = total.reshape(groups * some, 8, width)

        @pl.loop(1, leaves)
        def _(o):
            leaf_copy(h, o).start()

        mine[h] = slab[h, piece(l)]

    for k in range(done, seps):
        make_t(k)

    for h in range(halves):
        @pl.loop(1, leaves)
        def _(o):
            leaf_copy(h, o).wait()
            mine[h] += slab_in[h * (leaves - 1) + o - 1]

        @pl.loop(1, leaves)
        def _(o):
            back_copy(h, o).start()

        gathered[h, piece(l)] = mine[h]
        if h == 0:
            @pl.loop(0, chunks)
            def _(m):
                hi, lo = split(inverse_v[m].T)
                inv_hi[m] = hi
                inv_lo[m] = lo

    others[2].wait()
    base = jnp.concatenate([root_rhs_v[k] for k in range(seps)], axis=1)
    updates = []
    for h in range(halves):
        @pl.loop(1, leaves)
        def _(o):
            back_copy(h, o).wait()

        value = gathered[h].reshape(groups, some, 8, width)
        updates += [value[:, k].reshape(narrow, width) for k in range(some)]
    update = jnp.concatenate(updates, axis=1)
    pending = base - update
    block = 2 * width
    blocks = seps // 2
    hi, lo = split(pending)
    forward = []
    for b in range(blocks):
        at = pl.ds(b * block, block)
        upto = (b + 1) * block
        forward.append(
            mul((hi[:, :upto], lo[:, :upto]), (t_hi[at, 0:upto], t_lo[at, 0:upto]), NT)
        )
    hi, lo = split(jnp.concatenate(forward, axis=1))
    solution_parts = []
    for b in range(blocks):
        at = pl.ds(b * block, block)
        rest = pl.ds(b * block, (blocks - b) * block)
        solution_parts.append(
            mul((hi[:, b * block:], lo[:, b * block:]), (t_hi[rest, at], t_lo[rest, at]), NN)
        )
    for k in range(seps):
        part_k = solution_parts[k // 2][:, (k % 2) * width:(k % 2 + 1) * width]
        root_all[r, c, :, k] = part_k.reshape(groups, 8, width)

    root_copies = []
    for o in range(1, cols):
        to = turn(c, o, cols)
        copy = remote(root_all.at[r, c], root_all.at[r, c], root_sem, o - 1, at_col(to))
        copy.start()
        root_copies.append(copy)

    def root_pair(i, which):
        return remote(root_all.at[r, which], root_all.at[r, which], root_pair_sem, i, at_row(1 - r))

    pair_copies = [root_pair(0, c)]
    pair_copies[0].start()
    for k in range(seps):
        part_k = solution_parts[k // 2][:, (k % 2) * width:(k % 2 + 1) * width]
        root_out[k] = part_k
    for o in range(1, cols):
        root_copies[o - 1].wait()
        copy = root_pair(o, turn(c, cols - o, cols))
        copy.start()
        pair_copies.append(copy)

    def make_resid(half):
        at = pl.ds(pl.multiple_of(half * (nrhs // 2), 128), nrhs // 2)
        value = root_all[half]
        left = split(jnp.concatenate([value[:, :, k].reshape(nrhs // 2, width) for k in range(seps)], axis=1))
        right = (coup_hi[...].reshape(seps * width, rows), coup_lo[...].reshape(seps * width, rows))
        return turned[at, :] - mul(left, right)

    turned[pl.ds(pl.multiple_of(r * (nrhs // 2), 128), nrhs // 2), :] = make_resid(r)
    for copy in pair_copies:
        copy.wait()
    other = 1 - r
    turned[pl.ds(pl.multiple_of(other * (nrhs // 2), 128), nrhs // 2), :] = make_resid(other)
    hi, lo = split(turned[...].T)
    resid_hi[...] = hi
    resid_lo[...] = lo

    def make_part(b):
        part[b] = mul((inv_hi[b], inv_lo[b]), (resid_hi[...], resid_lo[...]))

    x = c + 1 - 2 * lax.rem(c, 2)
    y = turn(c, 2, cols)
    z = cols - 1 - c
    upper, lower = pl.ds(0, rows // 2), pl.ds(rows // 2, rows // 2)

    def fin_pair(t):
        return remote(part.at[t], part_in.at[t], fin_pair_sem, t, at_row(1 - r))

    def slot(t):
        return r * cols + t

    def ready(t):
        @pl.when(r == 0)
        def _():
            fin_pair(t).wait_recv()
            part[t] += part_in[t]

        @pl.when(r == 1)
        def _():
            make_part(cols + t)

    def if_any(nonzero):
        return pl.when(jnp.logical_or(r == 0, nonzero))

    sends = [
        (remote(part.at[slot(z), upper], relay_in.at[0], fin_sem, 0, at_col(x)), z < c, y < x),
        (remote(part.at[slot(z), lower], relay_in.at[1], fin_sem, 1, at_col(y)), z < c, x < y),
        (remote(part.at[slot(x), upper], part_cols.at[0, upper], fin_sem, 2, at_col(x)), x < c, c < x),
        (remote(part.at[slot(y), lower], part_cols.at[1, lower], fin_sem, 3, at_col(y)), y < c, c < y),
        (
            remote(part.at[slot(y), upper], part_cols.at[1, upper], fin_sem, 4, at_col(y)),
            jnp.logical_or(y < c, y < x), jnp.logical_or(c < y, c < z),
        ),
        (
            remote(part.at[slot(x), lower], part_cols.at[0, lower], fin_sem, 5, at_col(x)),
            jnp.logical_or(x < c, x < y), jnp.logical_or(c < x, c < z),
        ),
    ]

    def send(i):
        @if_any(sends[i][1])
        def _():
            sends[i][0].start()

    def receive(i, then):
        @if_any(sends[i][2])
        def _():
            sends[i][0].wait_recv()
            then()

    for t in (z, x, y, c):
        make_part(t)

        @pl.when(r == 1)
        def _():
            fin_pair(t).start()

    ready(z)
    send(0)
    send(1)
    ready(x)
    send(2)
    ready(y)
    send(3)

    def add_upper():
        part[slot(y), upper] += relay_in[0]

    def add_lower():
        part[slot(x), lower] += relay_in[1]

    receive(0, add_upper)
    send(4)
    receive(1, add_lower)
    send(5)
    ready(c)
    leaf_out[0] = part[slot(c)]

    def add_part(way, at):
        def add():
            leaf_out[0, at] += part_cols[way, at]

        return add

    receive(2, add_part(0, upper))
    receive(3, add_part(1, lower))
    receive(4, add_part(1, upper))
    receive(5, add_part(0, lower))
    for copy, nonzero, _ in sends:
        @if_any(nonzero)
        def _():
            copy.wait_send()

    @pl.when(r == 1)
    def _():
        for t in range(cols):
            fin_pair(t).wait_send()


def hand_over(leaf_ref, root_ref, leaf_out, root_out, sems):
    copies = []
    pieces = sems.shape[0] // 2
    deep = leaf_ref.shape[1] // pieces
    for i in range(pieces):
        at = pl.ds(i * deep, deep)
        copies.append(pltpu.make_async_copy(leaf_ref.at[:, at], leaf_out.at[:, at], sems.at[i]))
    deep = root_ref.shape[0] // pieces
    for i in range(pieces):
        at = pl.ds(i * deep, deep)
        copies.append(pltpu.make_async_copy(root_ref.at[at], root_out.at[at], sems.at[pieces + i]))
    for copy in copies:
        copy.start()
    for copy in copies:
        copy.wait()


def per_device(sizes, leaf_rhs, root_rhs, leaf_inverse, coupling, coupled, root_inverse, root_lower):
    leaves, cols, seps, width, order, rows, nrhs = sizes
    narrow = nrhs // (2 * cols)
    groups = narrow // 8
    halves = halves_of(groups, seps, leaves)
    some = seps // halves
    per = groups * some // leaves
    chunks = order // rows
    slab_shape = (groups, seps, 8, width)
    half_shape = (groups, some, 8, width)
    any_space = pl.BlockSpec(memory_space=pl.ANY)
    vmem = pl.BlockSpec(memory_space=pltpu.VMEM)
    smem = pl.BlockSpec(memory_space=pltpu.SMEM)
    total = seps * width
    V = pltpu.VMEM
    sem = lambda *shape: pltpu.SemaphoreType.DMA(shape)
    scratch = [
        V((chunks, rows, nrhs), F32), V((chunks, rows, rows), F32), V((seps, width, rows), F32),
        V((seps, narrow, width), F32), V((seps, width, width), F32), V((seps, seps, width, width), F32),
        V((rows, nrhs), F32), V((nrhs, rows), F32), V((nrhs, rows), BF16), V((nrhs, rows), BF16),
        V((seps, width, rows), BF16), V((seps, width, rows), BF16),
        V((chunks, rows, rows), BF16), V((chunks, rows, rows), BF16),
        V((total, total), BF16), V((total, total), BF16),
        V((2, halves, cols) + half_shape, F32), V((halves, cols) + half_shape, F32),
        V((halves, cols) + half_shape, F32), V((halves * (cols - 1),) + half_shape, F32),
        V((halves, groups * some, 8, width), F32), V((halves * (leaves - 1), per, 8, width), F32),
        V((halves, per, 8, width), F32), V((halves, groups * some, 8, width), F32),
        V((2, cols) + slab_shape, F32), V((rows, nrhs), BF16), V((rows, nrhs), BF16),
        V((2 * cols, rows, nrhs), F32), V((cols, rows, nrhs), F32), V((2, rows // 2, nrhs), F32),
        V((2, rows, nrhs), F32),
        sem(4), sem(chunks), sem(chunks),
        sem(2, halves), sem(2, halves * (cols - 1)), sem(2, halves * (leaves - 1)), sem(2, halves * (leaves - 1)),
        sem(2, cols - 1), sem(2, cols), sem(2, cols), sem(2, 6),
    ]
    leaf_result, root_result = pl.pallas_call(
        functools.partial(kernel, sizes),
        out_shape=(
            jax.ShapeDtypeStruct((1, rows, nrhs), F32),
            jax.ShapeDtypeStruct((seps, narrow, width), F32),
        ),
        in_specs=[any_space, any_space, any_space, any_space, smem, any_space, any_space],
        out_specs=(vmem, vmem),
        scratch_shapes=scratch,
        compiler_params=pltpu.CompilerParams(
            collective_id=0, has_side_effects=True, vmem_limit_bytes=56 * 1024 * 1024
        ),
    )(leaf_rhs, root_rhs.transpose(0, 2, 1), leaf_inverse, coupling, coupled, root_inverse, root_lower)
    leaf_result, root_result = pl.pallas_call(
        hand_over,
        out_shape=(
            jax.ShapeDtypeStruct(leaf_result.shape, F32),
            jax.ShapeDtypeStruct(root_result.shape, F32),
        ),
        in_specs=[any_space, any_space],
        out_specs=(any_space, any_space),
        scratch_shapes=[sem(8)],
        compiler_params=pltpu.CompilerParams(vmem_limit_bytes=60 * 1024 * 1024),
    )(leaf_result, root_result)
    return leaf_result, root_result.transpose(0, 2, 1)


def solution(mesh):
    in_specs = (
        P("leaf", None, None),
        P(None, None, ("row", "col")),
        P("leaf", ("row", "col"), None),
        P("leaf", None, None, ("row", "col")),
        P("leaf", None),
        P(),
        P(),
    )
    out_specs = (P("leaf", ("row", "col"), None), P(None, None, ("row", "col")))
    leaves, cols = mesh.shape["leaf"], mesh.shape["col"]

    def run(leaf_rhs, root_rhs, leaf_inverse, coupling, coupled, root_inverse, root_lower):
        seps, width, nrhs = root_rhs.shape
        order = leaf_rhs.shape[1]
        sizes = (leaves, cols, seps, width, order, order // (2 * cols), nrhs)
        mapped = jax.shard_map(
            functools.partial(per_device, sizes), mesh=mesh, in_specs=in_specs, out_specs=out_specs,
            check_vma=False,
        )
        return mapped(leaf_rhs, root_rhs, leaf_inverse, coupling, coupled, root_inverse, root_lower)

    return run
```

```python
import functools

import jax
import jax.numpy as jnp
from jax import lax
from jax.experimental import pallas as pl
from jax.experimental.pallas import tpu as pltpu
from jax.sharding import PartitionSpec as P

F32 = jnp.float32
BF16 = jnp.bfloat16
MESH = pl.DeviceIdType.MESH
NN = (((1,), (0,)), ((), ()))
NT = (((1,), (1,)), ((), ()))


def split(value):
    high = value.astype(BF16)
    return high, (value - high.astype(F32)).astype(BF16)


def mul(a, b, dims=NN):
    dot = functools.partial(lax.dot_general, dimension_numbers=dims, preferred_element_type=F32)
    return dot(a[0], b[0]) + (dot(a[0], b[1]) + dot(a[1], b[0]))


def halves_of(groups, seps, leaves):
    return 2 if (groups * seps // 2) % leaves == 0 else 1


def kernel(
    sizes,
    rhs_hbm, root_rhs_hbm, inverse_hbm, coupling_hbm, coupled_ref, root_inverse_hbm, root_lower_hbm,
    leaf_out, root_out,
    rhs_v, inverse_v, coupling_v, root_rhs_v, root_inverse_v, root_lower_v,
    solved, turned, turned_hi, turned_lo, coup_hi, coup_lo, inv_hi, inv_lo,
    t_hi, t_lo,
    term, pair_in, pair_sum, cols_relay, cols_in, slab, slab_in, mine, gathered,
    root_all, resid_hi, resid_lo, part, part_in, relay_in, part_cols,
    load_sem, rhs_sem, inv_sem,
    pair_sem, cols_sem, leaf_sem, back_sem, root_sem, root_pair_sem, fin_pair_sem, fin_sem,
):
    leaves, cols, seps, width, order, rows, nrhs = sizes
    narrow = nrhs // (2 * cols)
    groups = narrow // 8
    halves = halves_of(groups, seps, leaves)
    some = seps // halves
    per = groups * some // leaves
    step = rows
    chunks = order // step
    l = lax.axis_index("leaf")
    r = lax.axis_index("row")
    c = lax.axis_index("col")

    def turn(value, by, count):
        return lax.rem(value + by, count)

    x = c + 1 - 2 * lax.rem(c, 2)
    y = turn(c, 2, cols)
    z = cols - 1 - c
    first, second = pl.ds(0, groups // 2), pl.ds(groups // 2, groups // 2)

    def at_row(x):
        return {"leaf": l, "row": x, "col": c}

    def at_col(x):
        return {"leaf": l, "row": r, "col": x}

    def at_leaf(x):
        return {"leaf": x, "row": r, "col": c}

    def remote(src, dst, sem, i, where):
        return pltpu.make_async_remote_copy(
            src_ref=src, dst_ref=dst, send_sem=sem.at[0, i], recv_sem=sem.at[1, i],
            device_id=where, device_id_type=MESH,
        )

    def inv_load(m):
        return pltpu.make_async_copy(
            inverse_hbm.at[0, :, pl.ds(pl.multiple_of(m * step, 128), step)], inverse_v.at[m], inv_sem.at[m]
        )

    def rhs_load(m):
        return pltpu.make_async_copy(
            rhs_hbm.at[0, pl.ds(pl.multiple_of(m * step, 8), step), :], rhs_v.at[m], rhs_sem.at[m]
        )

    others = [
        pltpu.make_async_copy(coupling_hbm.at[0], coupling_v, load_sem.at[0]),
        pltpu.make_async_copy(root_inverse_hbm, root_inverse_v, load_sem.at[1]),
        pltpu.make_async_copy(root_rhs_hbm, root_rhs_v, load_sem.at[2]),
        pltpu.make_async_copy(root_lower_hbm, root_lower_v, load_sem.at[3]),
    ]
    for m in range(chunks):
        inv_load(m).start()
        rhs_load(m).start()
    for copy in others:
        copy.start()

    barrier = pltpu.get_barrier_semaphore()
    pl.semaphore_signal(barrier, inc=1, device_id=at_row(1 - r), device_id_type=MESH)
    for o in range(1, cols):
        pl.semaphore_signal(barrier, inc=1, device_id=at_col(turn(c, o, cols)), device_id_type=MESH)

    @pl.loop(1, leaves)
    def _(o):
        pl.semaphore_signal(barrier, inc=1, device_id=at_leaf(turn(l, o, leaves)), device_id_type=MESH)

    solved[...] = jnp.zeros_like(solved)

    @pl.loop(0, chunks)
    def _(m):
        inv_load(m).wait()
        rhs_load(m).wait()
        solved[...] += mul(split(inverse_v[m]), split(rhs_v[m]))

    turned[...] = solved[...].T
    hi, lo = split(turned[...])
    turned_hi[...] = hi
    turned_lo[...] = lo
    others[0].wait()
    for k in range(seps):
        hi, lo = split(coupling_v[k] * coupled_ref[0, k].astype(F32))
        coup_hi[k] = hi
        coup_lo[k] = lo

    def make_term(half, h):
        at = pl.ds(pl.multiple_of(half * (nrhs // 2), 128), nrhs // 2)
        left = (turned_hi[at, :], turned_lo[at, :])

        @pl.loop(0, some)
        def _(k):
            value = mul(left, (coup_hi[h * some + k], coup_lo[h * some + k]), NT)
            term[half, h, :, :, k] = value.reshape(cols, groups, 8, width)

    pair_starts = []
    for h in range(halves):
        make_term(1 - r, h)
        if h == 0:
            pl.semaphore_wait(barrier, cols + leaves - 1)
        copy = remote(term.at[1 - r, h], pair_in.at[h], pair_sem, h, at_row(1 - r))
        copy.start()
        pair_starts.append(copy)

    def cols_sends(h):
        def one(i, src, dst, to):
            return remote(src, dst, cols_sem, h * 6 + i, at_col(to))

        return [
            one(0, pair_sum.at[h, z, first], cols_relay.at[h, 0], x),
            one(1, pair_sum.at[h, z, second], cols_relay.at[h, 1], y),
            one(2, pair_sum.at[h, x, first], cols_in.at[h, 0, first], x),
            one(3, pair_sum.at[h, y, second], cols_in.at[h, 1, second], y),
            one(4, pair_sum.at[h, y, first], cols_in.at[h, 1, first], y),
            one(5, pair_sum.at[h, x, second], cols_in.at[h, 0, second], x),
        ]

    cols_copies = [cols_sends(h) for h in range(halves)]
    for h in range(halves):
        make_term(r, h)
        pair_starts[h].wait()
        for to in (z, x, y, c):
            pair_sum[h, to] = term[r, h, to] + pair_in[h, to]
        for i in range(4):
            cols_copies[h][i].start()

    for h in range(halves):
        cols_copies[h][0].wait_recv()
        pair_sum[h, y, first] += cols_relay[h, 0]
        cols_copies[h][4].start()
        cols_copies[h][1].wait_recv()
        pair_sum[h, x, second] += cols_relay[h, 1]
        cols_copies[h][5].start()

    others[1].wait()
    others[3].wait()

    def make_t(k):
        at = pl.ds(k * width, width)
        inv_k = root_inverse_v[k]
        if k:
            low = jnp.concatenate([root_lower_v[k, j] for j in range(k)], axis=1)
            known = (t_hi[0:k * width, 0:k * width], t_lo[0:k * width, 0:k * width])
            row = -mul(split(inv_k), split(mul(split(low), known)))
            hi, lo = split(row)
            t_hi[at, 0:k * width] = hi
            t_lo[at, 0:k * width] = lo
        hi, lo = split(inv_k)
        t_hi[at, at] = hi
        t_lo[at, at] = lo
        if k + 1 < seps:
            rest = pl.ds((k + 1) * width, (seps - 1 - k) * width)
            t_hi[at, rest] = jnp.zeros((width, (seps - 1 - k) * width), BF16)
            t_lo[at, rest] = jnp.zeros((width, (seps - 1 - k) * width), BF16)

    def piece(x):
        return pl.ds(x * per, per)

    def leaf_copy(h, o):
        to = turn(l, o, leaves)
        i = h * (leaves - 1) + o - 1
        return remote(slab.at[h, piece(to)], slab_in.at[i], leaf_sem, i, at_leaf(to))

    def back_copy(h, o):
        to = turn(l, o, leaves)
        i = h * (leaves - 1) + o - 1
        return remote(mine.at[h], gathered.at[h, piece(l)], back_sem, i, at_leaf(to))

    done = 0
    for h in range(halves):
        upto = seps if h == halves - 1 else min(5, seps)
        if h == halves - 1 and halves > 1:
            upto = seps - 1
        for k in range(done, upto):
            make_t(k)
        done = upto
        for i in range(2, 6):
            cols_copies[h][i].wait_recv()
        for i in range(6):
            cols_copies[h][i].wait_send()
        total = pair_sum[h, c] + cols_in[h, 0] + cols_in[h, 1]
        slab[h] = total.reshape(groups * some, 8, width)

        @pl.loop(1, leaves)
        def _(o):
            leaf_copy(h, o).start()

        mine[h] = slab[h, piece(l)]

    for k in range(done, seps):
        make_t(k)

    for h in range(halves):
        @pl.loop(1, leaves)
        def _(o):
            leaf_copy(h, o).wait()
            mine[h] += slab_in[h * (leaves - 1) + o - 1]

        @pl.loop(1, leaves)
        def _(o):
            back_copy(h, o).start()

        gathered[h, piece(l)] = mine[h]
        if h == 0:
            @pl.loop(0, chunks)
            def _(m):
                hi, lo = split(inverse_v[m].T)
                inv_hi[m] = hi
                inv_lo[m] = lo

    others[2].wait()
    base = jnp.concatenate([root_rhs_v[k] for k in range(seps)], axis=1)
    updates = []
    for h in range(halves):
        @pl.loop(1, leaves)
        def _(o):
            back_copy(h, o).wait()

        value = gathered[h].reshape(groups, some, 8, width)
        updates += [value[:, k].reshape(narrow, width) for k in range(some)]
    update = jnp.concatenate(updates, axis=1)
    pending = base - update
    block = 2 * width
    blocks = seps // 2
    hi, lo = split(pending)
    forward = []
    for b in range(blocks):
        at = pl.ds(b * block, block)
        upto = (b + 1) * block
        forward.append(
            mul((hi[:, :upto], lo[:, :upto]), (t_hi[at, 0:upto], t_lo[at, 0:upto]), NT)
        )
    hi, lo = split(jnp.concatenate(forward, axis=1))
    solution_parts = []
    for b in range(blocks):
        at = pl.ds(b * block, block)
        rest = pl.ds(b * block, (blocks - b) * block)
        solution_parts.append(
            mul((hi[:, b * block:], lo[:, b * block:]), (t_hi[rest, at], t_lo[rest, at]), NN)
        )
    for k in range(seps):
        part_k = solution_parts[k // 2][:, (k % 2) * width:(k % 2 + 1) * width]
        root_all[r, c, :, k] = part_k.reshape(groups, 8, width)

    def root_send(i, which, at, to):
        return remote(root_all.at[r, which, at], root_all.at[r, which, at], root_sem, i, at_col(to))

    root_copies = [
        root_send(0, c, first, x), root_send(1, c, second, y),
        root_send(2, c, second, x), root_send(3, c, first, y),
        root_send(4, x, first, y), root_send(5, y, second, x),
    ]
    for i in range(4):
        root_copies[i].start()

    pair_copies = [
        remote(root_all.at[r, which], root_all.at[r, which], root_pair_sem, i, at_row(1 - r))
        for i, which in enumerate((c, x, y, z))
    ]
    pair_copies[0].start()
    root_copies[0].wait_recv()
    root_copies[4].start()
    root_copies[1].wait_recv()
    root_copies[5].start()
    for k in range(seps):
        part_k = solution_parts[k // 2][:, (k % 2) * width:(k % 2 + 1) * width]
        root_out[k] = part_k
    root_copies[2].wait_recv()
    pair_copies[1].start()
    root_copies[3].wait_recv()
    pair_copies[2].start()
    root_copies[4].wait_recv()
    root_copies[5].wait_recv()
    pair_copies[3].start()
    for copy in root_copies:
        copy.wait_send()

    def make_resid(half):
        at = pl.ds(pl.multiple_of(half * (nrhs // 2), 128), nrhs // 2)
        value = root_all[half]
        left = split(jnp.concatenate([value[:, :, k].reshape(nrhs // 2, width) for k in range(seps)], axis=1))
        right = (coup_hi[...].reshape(seps * width, rows), coup_lo[...].reshape(seps * width, rows))
        return turned[at, :] - mul(left, right)

    turned[pl.ds(pl.multiple_of(r * (nrhs // 2), 128), nrhs // 2), :] = make_resid(r)
    for copy in pair_copies:
        copy.wait()
    other = 1 - r
    turned[pl.ds(pl.multiple_of(other * (nrhs // 2), 128), nrhs // 2), :] = make_resid(other)
    hi, lo = split(turned[...].T)
    resid_hi[...] = hi
    resid_lo[...] = lo

    def make_part(b):
        part[b] = mul((inv_hi[b], inv_lo[b]), (resid_hi[...], resid_lo[...]))

    upper, lower = pl.ds(0, rows // 2), pl.ds(rows // 2, rows // 2)

    def fin_pair(t):
        return remote(part.at[t], part_in.at[t], fin_pair_sem, t, at_row(1 - r))

    def slot(t):
        return r * cols + t

    def ready(t):
        @pl.when(r == 0)
        def _():
            fin_pair(t).wait_recv()
            part[t] += part_in[t]

        @pl.when(r == 1)
        def _():
            make_part(cols + t)

    def if_any(nonzero):
        return pl.when(jnp.logical_or(r == 0, nonzero))

    sends = [
        (remote(part.at[slot(z), upper], relay_in.at[0], fin_sem, 0, at_col(x)), z < c, y < x),
        (remote(part.at[slot(z), lower], relay_in.at[1], fin_sem, 1, at_col(y)), z < c, x < y),
        (remote(part.at[slot(x), upper], part_cols.at[0, upper], fin_sem, 2, at_col(x)), x < c, c < x),
        (remote(part.at[slot(y), lower], part_cols.at[1, lower], fin_sem, 3, at_col(y)), y < c, c < y),
        (
            remote(part.at[slot(y), upper], part_cols.at[1, upper], fin_sem, 4, at_col(y)),
            jnp.logical_or(y < c, y < x), jnp.logical_or(c < y, c < z),
        ),
        (
            remote(part.at[slot(x), lower], part_cols.at[0, lower], fin_sem, 5, at_col(x)),
            jnp.logical_or(x < c, x < y), jnp.logical_or(c < x, c < z),
        ),
    ]

    def send(i):
        @if_any(sends[i][1])
        def _():
            sends[i][0].start()

    def receive(i, then):
        @if_any(sends[i][2])
        def _():
            sends[i][0].wait_recv()
            then()

    for t in (z, x, y, c):
        make_part(t)

        @pl.when(r == 1)
        def _():
            fin_pair(t).start()

    ready(z)
    send(0)
    send(1)
    ready(x)
    send(2)
    ready(y)
    send(3)

    def add_upper():
        part[slot(y), upper] += relay_in[0]

    def add_lower():
        part[slot(x), lower] += relay_in[1]

    receive(0, add_upper)
    send(4)
    receive(1, add_lower)
    send(5)
    ready(c)
    leaf_out[0] = part[slot(c)]

    def add_part(way, at):
        def add():
            leaf_out[0, at] += part_cols[way, at]

        return add

    receive(2, add_part(0, upper))
    receive(3, add_part(1, lower))
    receive(4, add_part(1, upper))
    receive(5, add_part(0, lower))
    for copy, nonzero, _ in sends:
        @if_any(nonzero)
        def _():
            copy.wait_send()

    @pl.when(r == 1)
    def _():
        for t in range(cols):
            fin_pair(t).wait_send()


def hand_over(leaf_ref, root_ref, leaf_out, root_out):
    leaf_out[...] = leaf_ref[...]
    root_out[...] = root_ref[...]


def per_device(sizes, leaf_rhs, root_rhs, leaf_inverse, coupling, coupled, root_inverse, root_lower):
    leaves, cols, seps, width, order, rows, nrhs = sizes
    narrow = nrhs // (2 * cols)
    groups = narrow // 8
    halves = halves_of(groups, seps, leaves)
    some = seps // halves
    per = groups * some // leaves
    chunks = order // rows
    slab_shape = (groups, seps, 8, width)
    half_shape = (groups, some, 8, width)
    any_space = pl.BlockSpec(memory_space=pl.ANY)
    vmem = pl.BlockSpec(memory_space=pltpu.VMEM)
    smem = pl.BlockSpec(memory_space=pltpu.SMEM)
    total = seps * width
    V = pltpu.VMEM
    sem = lambda *shape: pltpu.SemaphoreType.DMA(shape)
    scratch = [
        V((chunks, rows, nrhs), F32), V((chunks, rows, rows), F32), V((seps, width, rows), F32),
        V((seps, narrow, width), F32), V((seps, width, width), F32), V((seps, seps, width, width), F32),
        V((rows, nrhs), F32), V((nrhs, rows), F32), V((nrhs, rows), BF16), V((nrhs, rows), BF16),
        V((seps, width, rows), BF16), V((seps, width, rows), BF16),
        V((chunks, rows, rows), BF16), V((chunks, rows, rows), BF16),
        V((total, total), BF16), V((total, total), BF16),
        V((2, halves, cols) + half_shape, F32), V((halves, cols) + half_shape, F32),
        V((halves, cols) + half_shape, F32),
        V((halves, 2, groups // 2, some, 8, width), F32), V((halves, 2) + half_shape, F32),
        V((halves, groups * some, 8, width), F32), V((halves * (leaves - 1), per, 8, width), F32),
        V((halves, per, 8, width), F32), V((halves, groups * some, 8, width), F32),
        V((2, cols) + slab_shape, F32), V((rows, nrhs), BF16), V((rows, nrhs), BF16),
        V((2 * cols, rows, nrhs), F32), V((cols, rows, nrhs), F32), V((2, rows // 2, nrhs), F32),
        V((2, rows, nrhs), F32),
        sem(4), sem(chunks), sem(chunks),
        sem(2, halves), sem(2, halves * 6), sem(2, halves * (leaves - 1)), sem(2, halves * (leaves - 1)),
        sem(2, 6), sem(2, cols), sem(2, cols), sem(2, 6),
    ]
    leaf_result, root_result = pl.pallas_call(
        functools.partial(kernel, sizes),
        out_shape=(
            jax.ShapeDtypeStruct((1, rows, nrhs), F32),
            jax.ShapeDtypeStruct((seps, narrow, width), F32),
        ),
        in_specs=[any_space, any_space, any_space, any_space, smem, any_space, any_space],
        out_specs=(vmem, vmem),
        scratch_shapes=scratch,
        compiler_params=pltpu.CompilerParams(
            collective_id=0, has_side_effects=True, vmem_limit_bytes=56 * 1024 * 1024
        ),
    )(leaf_rhs, root_rhs.transpose(0, 2, 1), leaf_inverse, coupling, coupled, root_inverse, root_lower)
    leaf_result, root_result = pl.pallas_call(
        hand_over,
        out_shape=(
            jax.ShapeDtypeStruct(leaf_result.shape, F32),
            jax.ShapeDtypeStruct(root_result.shape, F32),
        ),
        in_specs=[vmem, vmem],
        out_specs=(vmem, vmem),
        compiler_params=pltpu.CompilerParams(vmem_limit_bytes=60 * 1024 * 1024),
    )(leaf_result, root_result)
    return leaf_result, root_result.transpose(0, 2, 1)


def solution(mesh):
    in_specs = (
        P("leaf", None, None),
        P(None, None, ("row", "col")),
        P("leaf", ("row", "col"), None),
        P("leaf", None, None, ("row", "col")),
        P("leaf", None),
        P(),
        P(),
    )
    out_specs = (P("leaf", ("row", "col"), None), P(None, None, ("row", "col")))
    leaves, cols = mesh.shape["leaf"], mesh.shape["col"]

    def run(leaf_rhs, root_rhs, leaf_inverse, coupling, coupled, root_inverse, root_lower):
        seps, width, nrhs = root_rhs.shape
        order = leaf_rhs.shape[1]
        sizes = (leaves, cols, seps, width, order, order // (2 * cols), nrhs)
        mapped = jax.shard_map(
            functools.partial(per_device, sizes), mesh=mesh, in_specs=in_specs, out_specs=out_specs,
            check_vma=False,
        )
        return mapped(leaf_rhs, root_rhs, leaf_inverse, coupling, coupled, root_inverse, root_lower)

    return run
```

```python
import functools

import jax
import jax.numpy as jnp
from jax import lax
from jax.experimental import pallas as pl
from jax.experimental.pallas import tpu as pltpu
from jax.sharding import PartitionSpec as P

F32 = jnp.float32
BF16 = jnp.bfloat16
MESH = pl.DeviceIdType.MESH
NN = (((1,), (0,)), ((), ()))
NT = (((1,), (1,)), ((), ()))


def split(value):
    high = value.astype(BF16)
    return high, (value - high.astype(F32)).astype(BF16)


def mul(a, b, dims=NN):
    dot = functools.partial(lax.dot_general, dimension_numbers=dims, preferred_element_type=F32)
    return dot(a[0], b[0]) + (dot(a[0], b[1]) + dot(a[1], b[0]))


def halves_of(groups, seps, leaves):
    return 2 if (groups * seps // 2) % leaves == 0 else 1


def kernel(
    sizes,
    rhs_hbm, root_rhs_hbm, inverse_hbm, coupling_hbm, coupled_ref, root_inverse_hbm, root_lower_hbm,
    leaf_out, root_out,
    rhs_v, inverse_v, coupling_v, root_rhs_v, root_inverse_v, root_lower_v,
    solved, turned, turned_hi, turned_lo, coup_hi, coup_lo, inv_hi, inv_lo,
    t_hi, t_lo,
    term, pair_in, pair_sum, cols_in, slab, slab_in, mine, gathered,
    root_all, resid_hi, resid_lo, part, part_in, relay_in, part_cols,
    load_sem, rhs_sem, inv_sem,
    pair_sem, cols_sem, leaf_sem, back_sem, root_sem, root_pair_sem, fin_pair_sem, fin_sem,
):
    leaves, cols, seps, width, order, rows, nrhs = sizes
    narrow = nrhs // (2 * cols)
    groups = narrow // 8
    halves = halves_of(groups, seps, leaves)
    some = seps // halves
    per = groups * some // leaves
    step = rows
    chunks = order // step
    l = lax.axis_index("leaf")
    r = lax.axis_index("row")
    c = lax.axis_index("col")

    def turn(value, by, count):
        return lax.rem(value + by, count)

    def at_row(x):
        return {"leaf": l, "row": x, "col": c}

    def at_col(x):
        return {"leaf": l, "row": r, "col": x}

    def at_leaf(x):
        return {"leaf": x, "row": r, "col": c}

    def remote(src, dst, sem, i, where):
        return pltpu.make_async_remote_copy(
            src_ref=src, dst_ref=dst, send_sem=sem.at[0, i], recv_sem=sem.at[1, i],
            device_id=where, device_id_type=MESH,
        )

    def inv_load(m):
        return pltpu.make_async_copy(
            inverse_hbm.at[0, :, pl.ds(pl.multiple_of(m * step, 128), step)], inverse_v.at[m], inv_sem.at[m]
        )

    def rhs_load(m):
        return pltpu.make_async_copy(
            rhs_hbm.at[0, pl.ds(pl.multiple_of(m * step, 8), step), :], rhs_v.at[m], rhs_sem.at[m]
        )

    others = [
        pltpu.make_async_copy(coupling_hbm.at[0], coupling_v, load_sem.at[0]),
        pltpu.make_async_copy(root_inverse_hbm, root_inverse_v, load_sem.at[1]),
        pltpu.make_async_copy(root_rhs_hbm, root_rhs_v, load_sem.at[2]),
        pltpu.make_async_copy(root_lower_hbm, root_lower_v, load_sem.at[3]),
    ]
    for m in range(chunks):
        inv_load(m).start()
        rhs_load(m).start()
    others[0].start()

    barrier = pltpu.get_barrier_semaphore()
    pl.semaphore_signal(barrier, inc=1, device_id=at_row(1 - r), device_id_type=MESH)
    for o in range(1, cols):
        pl.semaphore_signal(barrier, inc=1, device_id=at_col(turn(c, o, cols)), device_id_type=MESH)

    @pl.loop(1, leaves)
    def _(o):
        pl.semaphore_signal(barrier, inc=1, device_id=at_leaf(turn(l, o, leaves)), device_id_type=MESH)

    solved[...] = jnp.zeros_like(solved)

    @pl.loop(0, chunks)
    def _(m):
        inv_load(m).wait()
        rhs_load(m).wait()
        solved[...] += mul(split(inverse_v[m]), split(rhs_v[m]))

    for copy in others[1:]:
        copy.start()
    turned[...] = solved[...].T
    hi, lo = split(turned[...])
    turned_hi[...] = hi
    turned_lo[...] = lo
    others[0].wait()
    for k in range(seps):
        hi, lo = split(coupling_v[k] * coupled_ref[0, k].astype(F32))
        coup_hi[k] = hi
        coup_lo[k] = lo

    def make_term(half, h):
        at = pl.ds(pl.multiple_of(half * (nrhs // 2), 128), nrhs // 2)
        left = (turned_hi[at, :], turned_lo[at, :])

        @pl.loop(0, some)
        def _(k):
            value = mul(left, (coup_hi[h * some + k], coup_lo[h * some + k]), NT)
            term[half, h, :, :, k] = value.reshape(cols, groups, 8, width)

    pair_starts = []
    for h in range(halves):
        make_term(1 - r, h)
        if h == 0:
            pl.semaphore_wait(barrier, cols + leaves - 1)
        copy = remote(term.at[1 - r, h], pair_in.at[h], pair_sem, h, at_row(1 - r))
        copy.start()
        pair_starts.append(copy)

    cols_copies = []
    for h in range(halves):
        make_term(r, h)
        pair_starts[h].wait()
        for o in range(1, cols):
            to = turn(c, o, cols)
            pair_sum[h, to] = term[r, h, to] + pair_in[h, to]
            i = h * (cols - 1) + o - 1
            copy = remote(pair_sum.at[h, to], cols_in.at[i], cols_sem, i, at_col(to))
            copy.start()
            cols_copies.append(copy)
        pair_sum[h, c] = term[r, h, c] + pair_in[h, c]

    others[1].wait()
    others[3].wait()

    def make_t(k):
        at = pl.ds(k * width, width)
        inv_k = root_inverse_v[k]
        if k:
            low = jnp.concatenate([root_lower_v[k, j] for j in range(k)], axis=1)
            known = (t_hi[0:k * width, 0:k * width], t_lo[0:k * width, 0:k * width])
            row = -mul(split(inv_k), split(mul(split(low), known)))
            hi, lo = split(row)
            t_hi[at, 0:k * width] = hi
            t_lo[at, 0:k * width] = lo
        hi, lo = split(inv_k)
        t_hi[at, at] = hi
        t_lo[at, at] = lo
        if k + 1 < seps:
            rest = pl.ds((k + 1) * width, (seps - 1 - k) * width)
            t_hi[at, rest] = jnp.zeros((width, (seps - 1 - k) * width), BF16)
            t_lo[at, rest] = jnp.zeros((width, (seps - 1 - k) * width), BF16)

    def piece(x):
        return pl.ds(x * per, per)

    def leaf_copy(h, o):
        to = turn(l, o, leaves)
        i = h * (leaves - 1) + o - 1
        return remote(slab.at[h, piece(to)], slab_in.at[i], leaf_sem, i, at_leaf(to))

    def back_copy(h, o):
        to = turn(l, o, leaves)
        i = h * (leaves - 1) + o - 1
        return remote(mine.at[h], gathered.at[h, piece(l)], back_sem, i, at_leaf(to))

    done = 0
    for h in range(halves):
        upto = seps if h == halves - 1 else min(5, seps)
        if h == halves - 1 and halves > 1:
            upto = seps - 1
        for k in range(done, upto):
            make_t(k)
        done = upto
        total = pair_sum[h, c]
        for o in range(1, cols):
            cols_copies[h * (cols - 1) + o - 1].wait()
            total = total + cols_in[h * (cols - 1) + o - 1]
        slab[h] = total.reshape(groups * some, 8, width)

        @pl.loop(1, leaves)
        def _(o):
            leaf_copy(h, o).start()

        mine[h] = slab[h, piece(l)]

    for k in range(done, seps):
        make_t(k)

    for h in range(halves):
        @pl.loop(1, leaves)
        def _(o):
            leaf_copy(h, o).wait()
            mine[h] += slab_in[h * (leaves - 1) + o - 1]

        @pl.loop(1, leaves)
        def _(o):
            back_copy(h, o).start()

        gathered[h, piece(l)] = mine[h]
        if h == 0:
            @pl.loop(0, chunks)
            def _(m):
                hi, lo = split(inverse_v[m].T)
                inv_hi[m] = hi
                inv_lo[m] = lo

    others[2].wait()
    base = jnp.concatenate([root_rhs_v[k] for k in range(seps)], axis=1)
    updates = []
    for h in range(halves):
        @pl.loop(1, leaves)
        def _(o):
            back_copy(h, o).wait()

        value = gathered[h].reshape(groups, some, 8, width)
        updates += [value[:, k].reshape(narrow, width) for k in range(some)]
    update = jnp.concatenate(updates, axis=1)
    pending = base - update
    block = 2 * width
    blocks = seps // 2
    hi, lo = split(pending)
    forward = []
    for b in range(blocks):
        at = pl.ds(b * block, block)
        upto = (b + 1) * block
        forward.append(
            mul((hi[:, :upto], lo[:, :upto]), (t_hi[at, 0:upto], t_lo[at, 0:upto]), NT)
        )
    hi, lo = split(jnp.concatenate(forward, axis=1))
    solution_parts = []
    for b in range(blocks):
        at = pl.ds(b * block, block)
        rest = pl.ds(b * block, (blocks - b) * block)
        solution_parts.append(
            mul((hi[:, b * block:], lo[:, b * block:]), (t_hi[rest, at], t_lo[rest, at]), NN)
        )
    for k in range(seps):
        part_k = solution_parts[k // 2][:, (k % 2) * width:(k % 2 + 1) * width]
        root_all[r, c, :, k] = part_k.reshape(groups, 8, width)

    root_copies = []
    for o in range(1, cols):
        to = turn(c, o, cols)
        copy = remote(root_all.at[r, c], root_all.at[r, c], root_sem, o - 1, at_col(to))
        copy.start()
        root_copies.append(copy)

    def root_pair(i, which):
        return remote(root_all.at[r, which], root_all.at[r, which], root_pair_sem, i, at_row(1 - r))

    pair_copies = [root_pair(0, c)]
    pair_copies[0].start()
    for k in range(seps):
        part_k = solution_parts[k // 2][:, (k % 2) * width:(k % 2 + 1) * width]
        root_out[k] = part_k
    for o in range(1, cols):
        root_copies[o - 1].wait()
        copy = root_pair(o, turn(c, cols - o, cols))
        copy.start()
        pair_copies.append(copy)

    def make_resid(half):
        at = pl.ds(pl.multiple_of(half * (nrhs // 2), 128), nrhs // 2)
        value = root_all[half]
        left = split(jnp.concatenate([value[:, :, k].reshape(nrhs // 2, width) for k in range(seps)], axis=1))
        right = (coup_hi[...].reshape(seps * width, rows), coup_lo[...].reshape(seps * width, rows))
        return turned[at, :] - mul(left, right)

    turned[pl.ds(pl.multiple_of(r * (nrhs // 2), 128), nrhs // 2), :] = make_resid(r)
    for copy in pair_copies:
        copy.wait()
    other = 1 - r
    turned[pl.ds(pl.multiple_of(other * (nrhs // 2), 128), nrhs // 2), :] = make_resid(other)
    hi, lo = split(turned[...].T)
    resid_hi[...] = hi
    resid_lo[...] = lo

    def make_part(b):
        part[b] = mul((inv_hi[b], inv_lo[b]), (resid_hi[...], resid_lo[...]))

    x = c + 1 - 2 * lax.rem(c, 2)
    y = turn(c, 2, cols)
    z = cols - 1 - c
    upper, lower = pl.ds(0, rows // 2), pl.ds(rows // 2, rows // 2)

    def fin_pair(t):
        return remote(part.at[t], part_in.at[t], fin_pair_sem, t, at_row(1 - r))

    def slot(t):
        return r * cols + t

    def ready(t):
        @pl.when(r == 0)
        def _():
            fin_pair(t).wait_recv()
            part[t] += part_in[t]

        @pl.when(r == 1)
        def _():
            make_part(cols + t)

    def if_any(nonzero):
        return pl.when(jnp.logical_or(r == 0, nonzero))

    sends = [
        (remote(part.at[slot(z), upper], relay_in.at[0], fin_sem, 0, at_col(x)), z < c, y < x),
        (remote(part.at[slot(z), lower], relay_in.at[1], fin_sem, 1, at_col(y)), z < c, x < y),
        (remote(part.at[slot(x), upper], part_cols.at[0, upper], fin_sem, 2, at_col(x)), x < c, c < x),
        (remote(part.at[slot(y), lower], part_cols.at[1, lower], fin_sem, 3, at_col(y)), y < c, c < y),
        (
            remote(part.at[slot(y), upper], part_cols.at[1, upper], fin_sem, 4, at_col(y)),
            jnp.logical_or(y < c, y < x), jnp.logical_or(c < y, c < z),
        ),
        (
            remote(part.at[slot(x), lower], part_cols.at[0, lower], fin_sem, 5, at_col(x)),
            jnp.logical_or(x < c, x < y), jnp.logical_or(c < x, c < z),
        ),
    ]

    def send(i):
        @if_any(sends[i][1])
        def _():
            sends[i][0].start()

    def receive(i, then):
        @if_any(sends[i][2])
        def _():
            sends[i][0].wait_recv()
            then()

    for t in (z, x, y, c):
        make_part(t)

        @pl.when(r == 1)
        def _():
            fin_pair(t).start()

    ready(z)
    send(0)
    send(1)
    ready(x)
    send(2)
    ready(y)
    send(3)

    def add_upper():
        part[slot(y), upper] += relay_in[0]

    def add_lower():
        part[slot(x), lower] += relay_in[1]

    receive(0, add_upper)
    send(4)
    receive(1, add_lower)
    send(5)
    ready(c)
    leaf_out[0] = part[slot(c)]

    def add_part(way, at):
        def add():
            leaf_out[0, at] += part_cols[way, at]

        return add

    receive(2, add_part(0, upper))
    receive(3, add_part(1, lower))
    receive(4, add_part(1, upper))
    receive(5, add_part(0, lower))
    for copy, nonzero, _ in sends:
        @if_any(nonzero)
        def _():
            copy.wait_send()

    @pl.when(r == 1)
    def _():
        for t in range(cols):
            fin_pair(t).wait_send()


def hand_over(leaf_ref, root_ref, leaf_out, root_out):
    leaf_out[...] = leaf_ref[...]
    root_out[...] = root_ref[...]


def per_device(sizes, leaf_rhs, root_rhs, leaf_inverse, coupling, coupled, root_inverse, root_lower):
    leaves, cols, seps, width, order, rows, nrhs = sizes
    narrow = nrhs // (2 * cols)
    groups = narrow // 8
    halves = halves_of(groups, seps, leaves)
    some = seps // halves
    per = groups * some // leaves
    chunks = order // rows
    slab_shape = (groups, seps, 8, width)
    half_shape = (groups, some, 8, width)
    any_space = pl.BlockSpec(memory_space=pl.ANY)
    vmem = pl.BlockSpec(memory_space=pltpu.VMEM)
    smem = pl.BlockSpec(memory_space=pltpu.SMEM)
    total = seps * width
    V = pltpu.VMEM
    sem = lambda *shape: pltpu.SemaphoreType.DMA(shape)
    scratch = [
        V((chunks, rows, nrhs), F32), V((chunks, rows, rows), F32), V((seps, width, rows), F32),
        V((seps, narrow, width), F32), V((seps, width, width), F32), V((seps, seps, width, width), F32),
        V((rows, nrhs), F32), V((nrhs, rows), F32), V((nrhs, rows), BF16), V((nrhs, rows), BF16),
        V((seps, width, rows), BF16), V((seps, width, rows), BF16),
        V((chunks, rows, rows), BF16), V((chunks, rows, rows), BF16),
        V((total, total), BF16), V((total, total), BF16),
        V((2, halves, cols) + half_shape, F32), V((halves, cols) + half_shape, F32),
        V((halves, cols) + half_shape, F32), V((halves * (cols - 1),) + half_shape, F32),
        V((halves, groups * some, 8, width), F32), V((halves * (leaves - 1), per, 8, width), F32),
        V((halves, per, 8, width), F32), V((halves, groups * some, 8, width), F32),
        V((2, cols) + slab_shape, F32), V((rows, nrhs), BF16), V((rows, nrhs), BF16),
        V((2 * cols, rows, nrhs), F32), V((cols, rows, nrhs), F32), V((2, rows // 2, nrhs), F32),
        V((2, rows, nrhs), F32),
        sem(4), sem(chunks), sem(chunks),
        sem(2, halves), sem(2, halves * (cols - 1)), sem(2, halves * (leaves - 1)), sem(2, halves * (leaves - 1)),
        sem(2, cols - 1), sem(2, cols), sem(2, cols), sem(2, 6),
    ]
    leaf_result, root_result = pl.pallas_call(
        functools.partial(kernel, sizes),
        out_shape=(
            jax.ShapeDtypeStruct((1, rows, nrhs), F32),
            jax.ShapeDtypeStruct((seps, narrow, width), F32),
        ),
        in_specs=[any_space, any_space, any_space, any_space, smem, any_space, any_space],
        out_specs=(vmem, vmem),
        scratch_shapes=scratch,
        compiler_params=pltpu.CompilerParams(
            collective_id=0, has_side_effects=True, vmem_limit_bytes=56 * 1024 * 1024
        ),
    )(leaf_rhs, root_rhs.transpose(0, 2, 1), leaf_inverse, coupling, coupled, root_inverse, root_lower)
    leaf_result, root_result = pl.pallas_call(
        hand_over,
        out_shape=(
            jax.ShapeDtypeStruct(leaf_result.shape, F32),
            jax.ShapeDtypeStruct(root_result.shape, F32),
        ),
        in_specs=[vmem, vmem],
        out_specs=(vmem, vmem),
        compiler_params=pltpu.CompilerParams(vmem_limit_bytes=60 * 1024 * 1024),
    )(leaf_result, root_result)
    return leaf_result, root_result.transpose(0, 2, 1)


def solution(mesh):
    in_specs = (
        P("leaf", None, None),
        P(None, None, ("row", "col")),
        P("leaf", ("row", "col"), None),
        P("leaf", None, None, ("row", "col")),
        P("leaf", None),
        P(),
        P(),
    )
    out_specs = (P("leaf", ("row", "col"), None), P(None, None, ("row", "col")))
    leaves, cols = mesh.shape["leaf"], mesh.shape["col"]

    def run(leaf_rhs, root_rhs, leaf_inverse, coupling, coupled, root_inverse, root_lower):
        seps, width, nrhs = root_rhs.shape
        order = leaf_rhs.shape[1]
        sizes = (leaves, cols, seps, width, order, order // (2 * cols), nrhs)
        mapped = jax.shard_map(
            functools.partial(per_device, sizes), mesh=mesh, in_specs=in_specs, out_specs=out_specs,
            check_vma=False,
        )
        return mapped(leaf_rhs, root_rhs, leaf_inverse, coupling, coupled, root_inverse, root_lower)

    return run
```
